512 devices in a mesh: dp: 64 (over z, y), head: 8 (over x, core).
Axes of the slice: x: 4, y: 4, z: 16, core: 2. Of those that a mesh axis runs over, the one named last changes fastest.
Arguments:
- query: bfloat16 [8192, 2048], P(('dp', 'head')), may hold values from -6 to 6
- key: bfloat16 [8192, 2048], P(('dp', 'head')), may hold values from -6 to 6
- value: bfloat16 [8192, 4096], P(('dp', 'head')), may hold values from -6 to 6
- beta_logit: float32 [8192, 32], P(('dp', 'head')), may hold values from -8 to 8
- decay: float32 [8192, 32], P(('dp', 'head')), may hold values from 0 to 1
- out_grad: bfloat16 [8192, 4096], P(('dp', 'head')), may hold values from -6 to 6
- ratio: float32 [8192], P(('dp', 'head')), may hold values from 0.5 to 2
- clip_mask: int32 [8192], P(('dp', 'head')), may hold values 0 or 1
- lengths: int32 [16], replicated, may hold values from 1 to 4096, 8192 in all
Outputs:
- query_grad: bfloat16 [8192, 2048], P(('dp', 'head'))
- key_grad: bfloat16 [8192, 2048], P(('dp', 'head'))
- value_grad: bfloat16 [8192, 4096], P(('dp', 'head'))
- beta_grad: float32 [8192, 32], P(('dp', 'head'))
- decay_grad: float32 [8192, 32], P(('dp', 'head'))
The draws below stay inside these ranges and needn't reach their ends.
Inputs may be any that keep to these rules, and one draw needn't show every extreme that they name: 16 lengths of at least 1 that sum to 8192; the longest is exactly 4096.
All inputs are finite; a program needn't handle non-finite values. No bound on the sum of `clip_mask` on one device may be relied on, other than what follows from the above.
Results may differ from the reference program's by a relative error of at most 0.0013.
Values may be sent and summed in bfloat16 or wider, within the bound.
A program may use at most 128 MiB of HBM per device.

```python
import math
import jax
import jax.numpy as jnp
import numpy as np
from jax import lax

QK_HEADS = 16
VALUE_HEAD_COUNT = 32
HEAD_DIM = 128
GROUP = 64
NSEQ = 16
TOKEN_TOTAL = 8192
MOST = 4096


def draw_beta_logit(key, part):
    key = jax.random.fold_in(key, 11)
    key_center, key_token = jax.random.split(key)
    centers = jax.random.uniform(key_center, (VALUE_HEAD_COUNT,), jnp.float32, -5.0, 2.0)
    spread = jax.random.normal(key_token, (TOKEN_TOTAL, VALUE_HEAD_COUNT), jnp.float32)
    return jnp.clip(centers[None, :] + spread, -8.0, 8.0)


def draw_decay(key, part):
    key = jax.random.fold_in(key, 7)
    key_speed, key_jagged, key_spike, key_length = jax.random.split(key, 4)
    log_low, log_high = (math.log(1e-05), math.log(0.03))
    decay_speeds = jnp.exp(jax.random.uniform(key_speed, (VALUE_HEAD_COUNT,), jnp.float32, log_low, log_high))
    jaggedness = jax.random.uniform(key_jagged, (TOKEN_TOTAL, VALUE_HEAD_COUNT), jnp.float32, 0.5, 2.0)
    spike_rows = (jax.random.uniform(key_spike, (TOKEN_TOTAL, 1), jnp.float32) < 4.0 / TOKEN_TOTAL).astype(jnp.float32)
    spike_length = jax.random.uniform(key_length, (TOKEN_TOTAL, VALUE_HEAD_COUNT), jnp.float32, 0.22, 0.69)
    return decay_speeds[None, :] * jaggedness + spike_rows * spike_length


def touch_ends(entries, key, low, largest):
    shape = entries.shape
    place = [jax.random.randint(jax.random.fold_in(key, axis), (), 0, shape[axis]) for axis in range(len(shape))]
    entries = entries.at[tuple(place)].set(low)
    longest = shape.index(max(shape))
    place[longest] = (place[longest] + 1) % shape[longest]
    return entries.at[tuple(place)].set(largest)


def shard_levels(own_key, dims, pieces, low, high):
    def one(dim, blocks):
        draws = jax.random.uniform(jax.random.fold_in(jax.random.fold_in(own_key, 6), dim), (blocks,), jnp.float32, low / len(pieces), high / len(pieces))
        return jnp.repeat(jnp.exp(draws), dims[dim] // blocks).reshape((-1,) + (1,) * (len(dims) - dim - 1))

    gain = one(*pieces[0])
    for cut in pieces[1:]:
        gain = gain * one(*cut)
    return gain


def length_profile(count, total, bound, lean):
    portions = [(1 << 20) // math.isqrt(standing ** lean) + 1 for standing in range(2, count + 1)]
    spare, counts = total - bound - (count - 1), [1] * (count - 1)
    while spare > 0:
        free = [i for i in range(count - 1) if counts[i] < bound]
        whole, budget = sum([portions[i] for i in free]), spare
        for i in free:
            addition = min(bound - counts[i], max(1, budget * portions[i] // whole), spare)
            counts[i] = counts[i] + addition
            spare = spare - addition
    return np.array([bound] + counts)


def uneven(stream_key, amount, total, most, skew):
    if amount == 2:
        one = jax.random.randint(stream_key, (), max(1, total - most), min(most, total - 1) + 1)
        return jnp.stack([one, total - one])
    sizes = jnp.asarray(length_profile(amount, total, most, skew), jnp.int32)
    couples = (amount - 1) // 2
    donor, taker = sizes[1:1 + 2 * couples:2], sizes[2:2 + 2 * couples:2]
    room = jnp.minimum(donor - 1, most - taker)
    passed = jax.random.randint(jax.random.fold_in(stream_key, 1), (couples,), 0, 1 << 20) % (room + 1)
    sizes = sizes.at[1:1 + 2 * couples:2].set(donor - passed).at[2:2 + 2 * couples:2].set(taker + passed)
    return sizes[jax.random.permutation(jax.random.fold_in(stream_key, 2), amount)]


def bell_draw(key, dims, scale, limit, shards=(), kind=jnp.bfloat16):
    array = jax.random.normal(key, dims, jnp.float32) * scale
    if len(shards) > 0:
        array = shard_levels(key, dims, shards, -0.22, 0.18) * array
    return jnp.clip(array, min=-limit, max=limit).astype(kind)


def setup_inputs(seed: int = 0) -> dict:
    key_of = jax.random.split(jax.random.key(seed), 10)
    query = bell_draw(key_of[0], (TOKEN_TOTAL, QK_HEADS * HEAD_DIM), 1.0, 6.0, ((0, 512),))
    key = bell_draw(key_of[1], (TOKEN_TOTAL, QK_HEADS * HEAD_DIM), 1.0, 6.0, ((0, 512),))
    value = bell_draw(key_of[2], (TOKEN_TOTAL, VALUE_HEAD_COUNT * HEAD_DIM), 1.0, 6.0, ((0, 512),))
    beta_logit = draw_beta_logit(jax.random.fold_in(key_of[9], 71), 0)
    decay = draw_decay(jax.random.fold_in(key_of[9], 71), 0)
    out_grad = bell_draw(key_of[5], (TOKEN_TOTAL, VALUE_HEAD_COUNT * HEAD_DIM), 1.0, 6.0, ((0, 512),))
    ratio = jnp.clip(jnp.exp(math.log(2.0) - 1.3862944 * jax.random.uniform(key_of[6], (TOKEN_TOTAL,), jnp.float32) ** shard_levels(key_of[6], (TOKEN_TOTAL,), ((0, 512),), -0.2, 0.2)), 0.5, 2.0)
    clip_mask = touch_ends((jax.random.randint(key_of[7], (TOKEN_TOTAL,), 0, 4) < 3).astype(jnp.int32), jax.random.fold_in(key_of[7], 1), 0, 1)
    lengths = uneven(key_of[8], NSEQ, TOKEN_TOTAL, MOST, 2).astype(jnp.int32)
    return dict(query=query, key=key, value=value, beta_logit=beta_logit, decay=decay, out_grad=out_grad, ratio=ratio, clip_mask=clip_mask, lengths=lengths)


exact_mode = lax.Precision.HIGHEST

def unit_rows(values):
    return values * lax.rsqrt(lax.optimization_barrier(jnp.sum(values * values, axis=-1, keepdims=True)) + 1e-06)

def segments(lengths, positions):
    doc_bounds = (jnp.cumsum(lengths) - lengths).astype(jnp.int32)
    doc_starts = jnp.any(positions[:, None] == doc_bounds[None, :], axis=1)
    doc_ids = lax.optimization_barrier(jnp.sum((doc_bounds[None, :] <= positions[:, None]).astype(jnp.int32), axis=1))
    return (doc_starts, doc_ids)

def group_step(state, block):
    q, k, v, beta, log_decay, doc_block, first_doc = block
    cumul = jnp.cumsum(log_decay, axis=-1)
    carried = (doc_block == first_doc).astype(jnp.float32)
    start_decay = jnp.exp(cumul) * carried[None, :]
    log_gap = cumul[:, :, None] - cumul[:, None, :]
    within = jnp.arange(GROUP, dtype=jnp.int32)
    same_doc = (doc_block[:, None] == doc_block[None, :]) & (within[:, None] >= within[None, :])
    pair_decay = jnp.where(same_doc[None], jnp.exp(jnp.minimum(log_gap, 0.0)), 0.0)
    strict = within[:, None] > within[None, :]
    key_gram = jnp.einsum('htd,hsd->hts', k, k, precision=exact_mode)
    tri_matrix = jnp.eye(GROUP, dtype=jnp.float32) + beta[:, :, None] * jnp.where(strict[None], pair_decay * key_gram, 0.0)
    solve_rhs = beta[:, :, None] * (v - start_decay[:, :, None] * jnp.einsum('htd,hde->hte', k, state, precision=exact_mode))
    writes = jax.scipy.linalg.solve_triangular(tri_matrix, solve_rhs, lower=True, unit_diagonal=True)
    query_key = jnp.einsum('htd,hsd->hts', q, k, precision=exact_mode)
    output = start_decay[:, :, None] * jnp.einsum('htd,hde->hte', q, state, precision=exact_mode)
    output = output + jnp.einsum('hts,hse->hte', pair_decay * query_key, writes, precision=exact_mode)
    end_decay = pair_decay[:, -1, :]
    new_state = start_decay[:, -1][:, None, None] * state
    new_state = new_state + jnp.einsum('hsd,hse->hde', k * end_decay[:, :, None], writes, precision=exact_mode)
    return (new_state, output)

def to_blocks(values, block_count):
    return jnp.swapaxes(values.reshape((block_count, GROUP) + values.shape[1:]), 1, 2)

def forward(query_f, key_f, value_f, beta_logit, decay, doc_starts, doc_ids):
    block_count = TOKEN_TOTAL // GROUP
    q = unit_rows(query_f.reshape(TOKEN_TOTAL, QK_HEADS, HEAD_DIM)) * HEAD_DIM ** (-0.5)
    k = unit_rows(key_f.reshape(TOKEN_TOTAL, QK_HEADS, HEAD_DIM))
    q = jnp.repeat(q, VALUE_HEAD_COUNT // QK_HEADS, axis=1)
    k = jnp.repeat(k, VALUE_HEAD_COUNT // QK_HEADS, axis=1)
    v = value_f.reshape(TOKEN_TOTAL, VALUE_HEAD_COUNT, HEAD_DIM)
    beta = jax.nn.sigmoid(beta_logit)
    doc_blocks = doc_ids.reshape(block_count, GROUP)
    first_docs = doc_blocks[:, 0] - doc_starts.reshape(block_count, GROUP)[:, 0].astype(jnp.int32)
    zero_state = jnp.zeros((VALUE_HEAD_COUNT, HEAD_DIM, HEAD_DIM), jnp.float32)
    inputs = (to_blocks(q, block_count), to_blocks(k, block_count), to_blocks(v, block_count), to_blocks(beta, block_count), to_blocks(-decay, block_count), doc_blocks, first_docs)
    final_state, outputs = lax.scan(jax.checkpoint(group_step), zero_state, inputs)
    return jnp.swapaxes(outputs, 1, 2).reshape(TOKEN_TOTAL, VALUE_HEAD_COUNT * HEAD_DIM)

def reference(query, key, value, beta_logit, decay, out_grad, ratio, clip_mask, lengths):
    positions = jnp.arange(TOKEN_TOTAL, dtype=jnp.int32)
    doc_starts, doc_ids = segments(lengths, positions)
    weight = ratio * clip_mask.astype(jnp.float32)
    cotangent = out_grad.astype(jnp.float32) * weight[:, None]

    def loss_value(query_f, key_f, value_f, beta_in, decay_in):
        output = forward(query_f, key_f, value_f, beta_in, decay_in, doc_starts, doc_ids)
        return jnp.sum(output * cotangent)
    grads = jax.grad(loss_value, argnums=(0, 1, 2, 3, 4))(query.astype(jnp.float32), key.astype(jnp.float32), value.astype(jnp.float32), beta_logit, decay)
    return (grads[0].astype(jnp.bfloat16), grads[1].astype(jnp.bfloat16), grads[2].astype(jnp.bfloat16), grads[3], grads[4])
```

```python
import functools

import jax
import jax.numpy as jnp
from jax import lax
from jax.experimental import pallas as pl
from jax.experimental.pallas import tpu as pltpu
from jax.sharding import PartitionSpec as P

HEAD_DIM = 128
TILE = 128
HEADS = 32
ROWS = 16
SPAN = HEADS * ROWS
TILES = SPAN // TILE
HOPS = 8
NDOCS = 16
SCALE = HEAD_DIM ** (-0.5)
MESH = pl.DeviceIdType.MESH
F32 = jnp.float32
BF16 = jnp.bfloat16
LIMIT = 56 * 1024 * 1024


def product(left, right, over=(1, 0)):
    return lax.dot_general(
        left, right, (((over[0],), (over[1],)), ((), ())), preferred_element_type=F32
    )


def halves(values):
    high = values.astype(BF16)
    return high, (values - high.astype(F32)).astype(BF16)


def thirds(values):
    high, rest = values.astype(BF16), None
    rest = values - high.astype(F32)
    middle = rest.astype(BF16)
    return high, middle, (rest - middle.astype(F32)).astype(BF16)


def product3(left, right, over=(1, 0)):
    (lh, ll), (rh, rl) = left, right
    return product(lh, rh, over) + (product(lh, rl, over) + product(ll, rh, over))


def product2l(left, right, over=(1, 0)):
    return product(left[0], right, over) + product(left[1], right, over)


def product2r(left, right, over=(1, 0)):
    return product(left, right[0], over) + product(left, right[1], over)


def iota(shape, axis):
    return lax.broadcasted_iota(jnp.int32, shape, axis)


def band(index):
    return slice(index * TILE, (index + 1) * TILE)


def place():
    dp, head = lax.axis_index("dp"), lax.axis_index("head")
    base = lax.div(dp, 4) * 4
    me = lax.rem(dp, 4) * 8 + head

    def device(index):
        return (base + lax.div(index, 8), lax.rem(index, 8))

    return dp, head, me, device


def greet_plane(me, device):
    barrier = pltpu.get_barrier_semaphore()

    def greet(offset, carry):
        target = lax.rem(me + offset, HEADS)
        pl.semaphore_signal(barrier, inc=1, device_id=device(target), device_id_type=MESH)
        return carry

    lax.fori_loop(1, HEADS, greet, 0)
    return barrier


def trade_plane(me, device, sent, landed, send_sem, recv_sem):
    def send(offset, carry):
        target = lax.rem(me + offset, HEADS)
        pltpu.make_async_remote_copy(
            src_ref=sent.at[target],
            dst_ref=landed.at[me],
            send_sem=send_sem,
            recv_sem=recv_sem,
            device_id=device(target),
            device_id_type=MESH,
        ).start()
        return carry

    lax.fori_loop(1, HEADS, send, 0)
    landed[me] = sent[me]
    others = pl.ds(0, HEADS - 1)
    pltpu.make_async_copy(sent.at[others], landed.at[others], recv_sem).wait()
    pltpu.make_async_copy(sent.at[others], landed.at[others], send_sem).wait()


def exchange_in(q_ref, k_ref, v_ref, g_ref, w_ref, out_ref, sent, landed, send_sem, recv_sem):
    _, _, me, device = place()
    barrier = greet_plane(me, device)
    parts = [p.astype(F32) for p in thirds(w_ref[...])]
    lane = iota((ROWS, TILE), 1) % 32
    for j in range(HEADS):
        pair = slice((j // 2) * HEAD_DIM, (j // 2 + 1) * HEAD_DIM)
        own = slice(j * HEAD_DIM, (j + 1) * HEAD_DIM)
        sent[j, 0:16, :] = q_ref[:, pair]
        sent[j, 16:32, :] = k_ref[:, pair]
        sent[j, 32:48, :] = v_ref[:, own]
        sent[j, 48:64, :] = g_ref[:, own]
        small = jnp.zeros((ROWS, TILE), F32)
        for n in range(3):
            moved = pltpu.roll(parts[n], (TILE - j + n) % TILE, 1)
            small = jnp.where(lane == n, moved, small)
        sent[j, 64:80, :] = small.astype(BF16)
    pl.semaphore_wait(barrier, HEADS - 1)
    trade_plane(me, device, sent, landed, send_sem, recv_sem)
    out_ref[...] = landed[...]


def raw_parts(in_ref):
    return [in_ref[:, n * 16 : n * 16 + 16, :].reshape(SPAN, TILE) for n in range(5)]


def local_first(
    lengths_ref, in_ref,
    phi_ref, phit_ref, bt_ref, lt_ref, u0_ref, wk_ref, x0_ref, xk_ref, gqk_ref, gkk_ref,
    vec_ref, a_ref, pw_ref, th_ref, tl_ref,
):
    base = lax.div(lax.axis_index("dp"), 4) * SPAN
    qr, kr, vr, gr, small = raw_parts(in_ref)
    qf, kf = qr.astype(F32), kr.astype(F32)
    pick_row, pick_col = iota((TILE, 3 * TILE), 0), iota((TILE, 3 * TILE), 1)
    pick = (pick_row // 32 == pick_col // TILE) & (pick_row % 32 < 3)
    spread = product(small, pick.astype(F32).astype(BF16))
    beta = jax.nn.sigmoid(spread[:, 0:TILE])
    weight = spread[:, 2 * TILE :]
    sk = lax.rsqrt(jnp.sum(kf * kf, axis=1, keepdims=True) + 1e-06)
    sk = jnp.broadcast_to(sk, (SPAN, TILE))
    csw = lax.rsqrt(jnp.sum(qf * qf, axis=1, keepdims=True) + 1e-06) * SCALE * weight
    lower = (iota((SPAN, SPAN), 0) >= iota((SPAN, SPAN), 1)).astype(F32).astype(BF16)
    running = product(lower, small)
    lane = iota((SPAN, TILE), 1)
    running = jnp.where(lane // 32 == 1, running, 0.0)
    cumul = -jnp.broadcast_to(jnp.sum(running, axis=1, keepdims=True), (SPAN, TILE))
    start = jnp.full((SPAN, TILE), -base, jnp.int32)
    last_start = -base
    row = iota((SPAN, TILE), 0)
    bound = -base
    for n in range(NDOCS - 1):
        bound = bound + lengths_ref[n]
        start = jnp.where(row >= bound, bound, start)
        last_start = jnp.where(bound <= SPAN - 1, bound, last_start)
    gamma = jnp.where(start < 0, jnp.exp(cumul), 0.0)
    last = cumul[SPAN - 1 : SPAN, :]
    end = jnp.where(row >= last_start, jnp.exp(jnp.minimum(last - cumul, 0.0)), 0.0)
    vec_ref[0] = beta
    vec_ref[1] = gamma
    vec_ref[2] = csw
    vec_ref[3] = sk
    vec_ref[4] = end
    pack = jnp.where(lane == 0, cumul, jnp.where(lane == 1, sk, 0.0))
    across = jnp.transpose(pack)
    tok, src = iota((TILE, TILE), 0), iota((TILE, TILE), 1)
    for i in range(TILES):
        bi = band(i)
        for j in range(i + 1):
            bj = band(j)
            gap = cumul[bi] - across[0:1, bj]
            seen = src + j * TILE >= start[bi]
            if i == j:
                seen = seen & (tok >= src)
            pair = jnp.where(seen, jnp.exp(jnp.minimum(gap, 0.0)), 0.0) * across[1:2, bj]
            gqk = pair * csw[bi]
            gkk = pair * (beta[bi] * sk[bi])
            if i == j:
                gkk = jnp.where(tok > src, gkk, 0.0)
            gqk_ref[bi, bj] = gqk
            gkk_ref[bi, bj] = gkk
            a_ref[bi, bj] = gkk * product(kr[bi], kr[bj], (1, 1))
            pw_ref[bi, bj] = gqk * product(qr[bi], kr[bj], (1, 1))
    eye = (tok == src).astype(F32)
    inverse = [eye - jnp.where(tok // 2 == src // 2, a_ref[band(i), band(i)], 0.0) for i in range(TILES)]
    size = 2
    while size < TILE:
        inside = (tok // (2 * size) == src // (2 * size)) & (tok // size != src // size)
        for i in range(TILES):
            block = halves(jnp.where(inside, a_ref[band(i), band(i)], 0.0))
            parts = halves(inverse[i])
            inverse[i] = inverse[i] - product3(parts, halves(product3(block, parts)))
        size *= 2
    for i in range(TILES):
        th_ref[band(i), band(i)], tl_ref[band(i), band(i)] = halves(inverse[i])
    size = TILE
    while size < SPAN:
        for n in range(SPAN // (2 * size)):
            top = slice(2 * n * size, (2 * n + 1) * size)
            low = slice((2 * n + 1) * size, (2 * n + 2) * size)
            right = product3(halves(a_ref[low, top]), (th_ref[top, top], tl_ref[top, top]))
            block = -product3((th_ref[low, low], tl_ref[low, low]), halves(right))
            th_ref[low, top], tl_ref[low, top] = halves(block)
            th_ref[top, low] = jnp.zeros((size, size), BF16)
            tl_ref[top, low] = jnp.zeros((size, size), BF16)
        size *= 2
    keys = sk * kf
    rhs = halves(jnp.concatenate([beta * vr.astype(F32), beta * gamma * keys], axis=1))
    solved = []
    for i in range(TILES):
        bi, upto = band(i), slice(0, (i + 1) * TILE)
        part = product3((th_ref[bi, upto], tl_ref[bi, upto]), (rhs[0][upto], rhs[1][upto]))
        u0_ref[bi] = part[:, :TILE]
        wk_ref[bi] = part[:, TILE:]
        solved.append(part)
    solved = halves(jnp.concatenate(solved, axis=0))
    end_keys = end * keys
    ends = halves(end_keys)
    both = product3(solved, ends, (0, 0))
    bt_ref[...] = both[:TILE]
    phit = gamma[SPAN - 1 : SPAN, :] * eye - both[TILE:]
    phit_ref[...] = phit
    phi_ref[...] = jnp.transpose(phit)
    wks = (solved[0][:, TILE:], solved[1][:, TILE:])
    reads = []
    for i in range(TILES):
        bi, upto = band(i), slice(0, (i + 1) * TILE)
        part = product3(halves(pw_ref[bi, upto]), (wks[0][upto], wks[1][upto]))
        reads.append(gamma[bi] * csw[bi] * qf[bi] - part)
    lt_ref[...] = product2r(gr, halves(jnp.concatenate(reads, axis=0)), (0, 0))
    pulled = []
    for j in range(TILES):
        bj, onward = band(j), slice(j * TILE, SPAN)
        pulled.append(product2l(halves(pw_ref[onward, bj]), gr[onward], (0, 0)))
    pulled = halves(jnp.concatenate([jnp.concatenate(pulled, axis=0), end_keys], axis=1))
    for j in range(TILES):
        bj, onward = band(j), slice(j * TILE, SPAN)
        part = product3(
            (th_ref[onward, bj], tl_ref[onward, bj]), (pulled[0][onward], pulled[1][onward]), (0, 0)
        )
        x0_ref[bj] = part[:, :TILE]
        xk_ref[bj] = part[:, TILE:]


def relay(
    phi_ref, phit_ref, bt_ref, lt_ref, state_ref, grad_ref,
    state_in, grad_in, state_out, grad_out, send_sems, recv_sems,
):
    dp, head = lax.axis_index("dp"), lax.axis_index("head")
    count = lax.axis_size("dp")
    after = (lax.rem(dp + 4, count), head)
    before = (lax.rem(dp + count - 4, count), head)
    barrier = pltpu.get_barrier_semaphore()
    for neighbour in (after, before):
        pl.semaphore_signal(barrier, inc=1, device_id=neighbour, device_id_type=MESH)
    pl.semaphore_wait(barrier, 2)
    phi, phit = halves(phi_ref[...]), halves(phit_ref[...])

    def copy(way, step):
        source, target = ((state_out, state_in), (grad_out, grad_in))[way]
        return pltpu.make_async_remote_copy(
            src_ref=source.at[step],
            dst_ref=target.at[step],
            send_sem=send_sems.at[way, step],
            recv_sem=recv_sems.at[way, step],
            device_id=(after, before)[way],
            device_id_type=MESH,
        )

    copies = []
    for step in range(HOPS):
        for way in range(2):
            local = (bt_ref, lt_ref)[way]
            if step == 0:
                value = local[...]
            else:
                copies[-2].wait_recv()
                arrived = (state_in, grad_in)[way][step - 1]
                value = product3(halves(arrived), (phit, phi)[way]) + local[...]
            (state_out, grad_out)[way][step] = value
            copies.append(copy(way, step))
            copies[-1].start()
    copies[-2].wait_recv()
    copies[-1].wait_recv()
    state_ref[...] = state_in[HOPS - 1]
    grad_ref[...] = grad_in[HOPS - 1]
    for one in copies:
        one.wait_send()


def local_second(
    in_ref, state_ref, grad_ref, phit_ref, bt_ref, u0_ref, wk_ref, x0_ref, xk_ref, gqk_ref, gkk_ref,
    vec_ref, dirs_ref, dv_ref, small_ref, fqh_ref, fql_ref, fkh_ref, fkl_ref,
):
    _, _, me, _ = place()
    qr, kr, vr, gr, _ = raw_parts(in_ref)
    beta, gamma, csw, sk, end = [vec_ref[n] for n in range(5)]
    state, grad = halves(state_ref[...]), halves(grad_ref[...])
    u = u0_ref[...] - product3(halves(wk_ref[...]), state, (1, 1))
    x = x0_ref[...] + product3(halves(xk_ref[...]), grad, (1, 1))
    dv = beta * x
    dv_ref[...] = dv.astype(BF16)
    (uh, ul), (xh, xl) = halves(u), halves(x)
    for i in range(TILES):
        bi = band(i)
        for j in range(i + 1):
            bj = band(j)
            read = product2r(gr[bi], (uh[bj], ul[bj]), (1, 1))
            solve = product3((xh[bi], xl[bi]), (uh[bj], ul[bj]), (1, 1))
            fqh_ref[bi, bj], fql_ref[bi, bj] = halves(gqk_ref[bi, bj] * read)
            fkh_ref[bi, bj], fkl_ref[bi, bj] = halves(-gkk_ref[bi, bj] * solve)
    dq = csw * gamma * product2r(gr, state)
    dk = end * sk * product3((uh, ul), grad) - beta * gamma * sk * product3((xh, xl), state)
    dqs, dks = [], []
    for i in range(TILES):
        bi, upto, onward = band(i), slice(0, (i + 1) * TILE), slice(i * TILE, SPAN)
        dqs.append(dq[bi] + product2l((fqh_ref[bi, upto], fql_ref[bi, upto]), kr[upto]))
        part = product2l((fqh_ref[onward, bi], fql_ref[onward, bi]), qr[onward], (0, 0))
        part = part + product2l((fkh_ref[onward, bi], fkl_ref[onward, bi]), kr[onward], (0, 0))
        part = part + product2l((fkh_ref[bi, upto], fkl_ref[bi, upto]), kr[upto])
        dks.append(dk[bi] + part)
    dq, dk = jnp.concatenate(dqs, axis=0), jnp.concatenate(dks, axis=0)
    dirs_ref[0] = dq
    dirs_ref[1] = dk
    after = product3(state, halves(phit_ref[...])) + bt_ref[...]
    total = jnp.sum(jnp.sum(grad_ref[...] * after, axis=1, keepdims=True), axis=0, keepdims=True)
    xu = jnp.sum(x * u, axis=1, keepdims=True)
    cumul = jnp.sum(
        qr.astype(F32) * dq - kr.astype(F32) * dk - 2.0 * (vr.astype(F32) * dv), axis=1, keepdims=True
    )
    cumul = cumul + 2.0 * xu
    cumul = jnp.where(iota((SPAN, 1), 0) == SPAN - 1, cumul + total, cumul)
    lane = iota((SPAN, TILE), 1)
    cumul = jnp.broadcast_to(cumul, (SPAN, TILE))
    pieces = [p.astype(F32) for p in thirds(cumul)]
    packed = jnp.zeros((SPAN, TILE), F32)
    for n in range(3):
        packed = jnp.where(lane == n, pieces[n], packed)
    upper = (iota((SPAN, SPAN), 0) <= iota((SPAN, SPAN), 1)).astype(F32).astype(BF16)
    ddecay = -jnp.sum(product(upper, packed.astype(BF16)), axis=1, keepdims=True)
    dbeta = xu * (1.0 - beta)
    ddecay = jnp.broadcast_to(ddecay, (SPAN, TILE))
    out = jnp.zeros((SPAN, TILE), F32)
    for n, values in enumerate((dbeta, ddecay)):
        high, low = halves(values)
        out = jnp.where(lane == me + 32 * n, high.astype(F32), out)
        out = jnp.where(lane == me + 32 * n + 64, low.astype(F32), out)
    small_ref[...] = out.astype(BF16)


def exchange_out(
    in_ref, dirs_ref, dv_ref, small_ref, dq_ref, dk_ref, dvo_ref, db_ref, dd_ref,
    partner_in, sent, landed, send_sem, recv_sem, pair_send, pair_recv,
):
    dp, head, me, device = place()
    core = lax.rem(head, 2)
    barrier = greet_plane(me, device)
    pl.semaphore_wait(barrier, HEADS - 1)
    pair = pltpu.make_async_remote_copy(
        src_ref=dirs_ref.at[1 - core],
        dst_ref=partner_in,
        send_sem=pair_send,
        recv_sem=pair_recv,
        device_id=(dp, head + 1 - 2 * core),
        device_id_type=MESH,
    )
    pair.start()
    own = jnp.where(core == 0, in_ref[:, 0:16, :], in_ref[:, 16:32, :]).reshape(SPAN, TILE)
    own = own.astype(F32)
    inverse = 1.0 / (jnp.sum(own * own, axis=1, keepdims=True) + 1e-06)
    sent[:, 16:32, :] = dv_ref[...].reshape(HEADS, ROWS, TILE)
    sent[:, 32:48, :] = small_ref[...].reshape(HEADS, ROWS, TILE)
    pair.wait_recv()
    grad = dirs_ref[core] + partner_in[...]
    grad = grad - own * (jnp.sum(own * grad, axis=1, keepdims=True) * inverse)
    sent[:, 0:16, :] = grad.astype(BF16).reshape(HEADS, ROWS, TILE)
    trade_plane(me, device, sent, landed, send_sem, recv_sem)
    total = jnp.zeros((ROWS, TILE), F32)
    for j in range(HEADS):
        to_ref = (dq_ref, dk_ref)[j % 2]
        to_ref[:, (j // 2) * HEAD_DIM : (j // 2 + 1) * HEAD_DIM] = landed[j, 0:16, :]
        dvo_ref[:, j * HEAD_DIM : (j + 1) * HEAD_DIM] = landed[j, 16:32, :]
        total = total + landed[j, 32:48, :].astype(F32)
    total = total + pltpu.roll(total, 64, 1)
    db_ref[...] = total[:, 0:32]
    dd_ref[...] = total[:, 32:64]
    pair.wait_send()


def call(body, outs, scratch, collective=None, smem=False, n_in=0, flops=0, name=None):
    vmem = pl.BlockSpec(memory_space=pltpu.VMEM)
    in_specs = [vmem] * n_in
    if smem:
        in_specs = [pl.BlockSpec(memory_space=pltpu.SMEM)] + in_specs[1:]
    if collective is None:
        params = pltpu.CompilerParams(vmem_limit_bytes=LIMIT)
    else:
        params = pltpu.CompilerParams(
            vmem_limit_bytes=LIMIT, collective_id=collective, has_side_effects=True
        )
    return pl.pallas_call(
        body,
        out_shape=[jax.ShapeDtypeStruct(s, d) for s, d in outs],
        in_specs=in_specs,
        out_specs=[vmem] * len(outs),
        scratch_shapes=scratch,
        compiler_params=params,
        cost_estimate=pl.CostEstimate(flops=flops, bytes_accessed=1 << 20, transcendentals=0),
        name=name,
    )


def shards(query, key, value, beta_logit, decay, out_grad, ratio, clip_mask, lengths):
    weight = ratio * clip_mask.astype(F32)
    wide = jnp.broadcast_to(weight[:, None], (ROWS, 64))
    columns = jnp.concatenate([beta_logit, decay, wide], axis=1)
    dma = pltpu.SemaphoreType.DMA
    square, tall, big = (TILE, TILE), (SPAN, TILE), (SPAN, SPAN)
    block_in = (HEADS, 80, TILE)
    (rows,) = call(
        exchange_in,
        [(block_in, BF16)],
        [pltpu.VMEM(block_in, BF16), pltpu.VMEM(block_in, BF16), dma, dma],
        collective=0,
        n_in=5,
        name="exchange_in",
    )(query, key, value, out_grad, columns)
    first = call(
        local_first,
        [(square, F32)] * 4 + [(tall, F32)] * 4 + [(big, F32)] * 2 + [((5,) + tall, F32)],
        [pltpu.VMEM(big, F32), pltpu.VMEM(big, F32), pltpu.VMEM(big, BF16), pltpu.VMEM(big, BF16)],
        n_in=2,
        smem=True,
        name="local_first",
    )(lengths, rows)
    phi, phit, bt, lt, u0, wk, x0, xk, gqk, gkk, vec = first
    slots = pltpu.VMEM((HOPS,) + square, F32)
    state, grad = call(
        relay,
        [(square, F32)] * 2,
        [slots] * 4 + [dma((2, HOPS)), dma((2, HOPS))],
        collective=1,
        n_in=4,
        name="relay",
    )(phi, phit, bt, lt)
    dirs, dv, small = call(
        local_second,
        [((2,) + tall, F32), (tall, BF16), (tall, BF16)],
        [pltpu.VMEM(big, BF16)] * 4,
        n_in=12,
        name="local_second",
    )(rows, state, grad, phit, bt, u0, wk, x0, xk, gqk, gkk, vec)
    block_out = (HEADS, 48, TILE)
    wide_out = HEADS * HEAD_DIM
    return tuple(
        call(
            exchange_out,
            [
                ((ROWS, wide_out // 2), BF16),
                ((ROWS, wide_out // 2), BF16),
                ((ROWS, wide_out), BF16),
                ((ROWS, HEADS), F32),
                ((ROWS, HEADS), F32),
            ],
            [pltpu.VMEM(tall, F32), pltpu.VMEM(block_out, BF16), pltpu.VMEM(block_out, BF16)]
            + [dma] * 4,
            collective=2,
            n_in=4,
            name="exchange_out",
        )(rows, dirs, dv, small)
    )


def solution(mesh):
    split = P(("dp", "head"), None)
    line = P(("dp", "head"))
    return jax.shard_map(
        shards,
        mesh=mesh,
        in_specs=(split,) * 6 + (line, line, P()),
        out_specs=(split,) * 5,
        check_vma=False,
    )
```

```python
import jax
import jax.numpy as jnp
from jax import lax
from jax.experimental import pallas as pl
from jax.experimental.pallas import tpu as pltpu
from jax.sharding import PartitionSpec as P

HEAD_DIM = 128
TILE = 128
HEADS = 32
ROWS = 16
SPAN = HEADS * ROWS
TILES = SPAN // TILE
REACH = (1, 2, 3)
NDOCS = 16
SCALE = HEAD_DIM ** (-0.5)
MESH = pl.DeviceIdType.MESH
F32 = jnp.float32
BF16 = jnp.bfloat16
LIMIT = 56 * 1024 * 1024


def product(left, right, over=(1, 0)):
    return lax.dot_general(
        left, right, (((over[0],), (over[1],)), ((), ())), preferred_element_type=F32
    )


def halves(values):
    high = values.astype(BF16)
    return high, (values - high.astype(F32)).astype(BF16)


def thirds(values):
    high, rest = values.astype(BF16), None
    rest = values - high.astype(F32)
    middle = rest.astype(BF16)
    return high, middle, (rest - middle.astype(F32)).astype(BF16)


def product3(left, right, over=(1, 0)):
    (lh, ll), (rh, rl) = left, right
    return product(lh, rh, over) + (product(lh, rl, over) + product(ll, rh, over))


def product2l(left, right, over=(1, 0)):
    return product(left[0], right, over) + product(left[1], right, over)


def product2r(left, right, over=(1, 0)):
    return product(left, right[0], over) + product(left, right[1], over)


def iota(shape, axis):
    return lax.broadcasted_iota(jnp.int32, shape, axis)


def band(index):
    return slice(index * TILE, (index + 1) * TILE)


def place():
    dp, head = lax.axis_index("dp"), lax.axis_index("head")
    base = lax.div(dp, 4) * 4
    me = lax.rem(dp, 4) * 8 + head

    def device(index):
        return (base + lax.div(index, 8), lax.rem(index, 8))

    return dp, head, me, device


def greet_plane(me, device):
    barrier = pltpu.get_barrier_semaphore()

    def greet(offset, carry):
        target = lax.rem(me + offset, HEADS)
        pl.semaphore_signal(barrier, inc=1, device_id=device(target), device_id_type=MESH)
        return carry

    lax.fori_loop(1, HEADS, greet, 0)
    return barrier


def start_plane(me, device, sent, landed, send_sem, recv_sem):
    def send(offset, carry):
        target = lax.rem(me + offset, HEADS)
        pltpu.make_async_remote_copy(
            src_ref=sent.at[target],
            dst_ref=landed.at[me],
            send_sem=send_sem,
            recv_sem=recv_sem,
            device_id=device(target),
            device_id_type=MESH,
        ).start()
        return carry

    lax.fori_loop(1, HEADS, send, 0)
    landed[me] = sent[me]


def finish_plane(sent, landed, send_sem, recv_sem):
    others = pl.ds(0, HEADS - 1)
    pltpu.make_async_copy(sent.at[others], landed.at[others], recv_sem).wait()
    pltpu.make_async_copy(sent.at[others], landed.at[others], send_sem).wait()


def raw_parts(landed):
    return [landed[:, n * 16 : n * 16 + 16, :].reshape(SPAN, TILE) for n in range(5)]


def whole(
    q_ref, k_ref, v_ref, g_ref, beta_ref, decay_ref, ratio_ref, clip_ref, lengths_ref,
    out_ref,
    sent_in, in_ref, columns_ref, lower_ref, upper_ref, start_ref, end_ref,
    u0_ref, wk_ref, x0_ref, xk_ref, gqk_ref, gkk_ref, a_ref, pw_ref, th_ref, tl_ref,
    fqh_ref, fql_ref, fkh_ref, fkl_ref, dirs_ref, partner_in, sent_out, landed,
    maps_out, maps_in, far_out, far_in, plane_send, plane_recv, out_send, out_recv,
    pair_send, pair_recv, map_send, map_recv,
):
    dp, head, me, device = place()
    count, core = lax.axis_size("dp"), lax.rem(head, 2)

    def along(distance):
        return (lax.rem(dp + (count + 4 * distance), count), head)

    barrier = greet_plane(me, device)
    for distance in REACH:
        for sign in (1, -1):
            pl.semaphore_signal(
                barrier, inc=1, device_id=along(sign * distance), device_id_type=MESH
            )

    columns_ref[...] = jnp.zeros((ROWS, TILE), F32)
    columns_ref[:, 0:32] = beta_ref[...]
    columns_ref[:, 32:64] = decay_ref[...]
    weight = ratio_ref[...] * clip_ref[...].astype(F32)
    diagonal = iota((ROWS, ROWS), 0) == iota((ROWS, ROWS), 1)
    weight = jnp.sum(jnp.where(diagonal, jnp.broadcast_to(weight, (ROWS, ROWS)), 0.0), axis=1, keepdims=True)
    wide = iota((ROWS, TILE), 1) >= 64
    columns = jnp.where(wide, jnp.broadcast_to(weight, (ROWS, TILE)), columns_ref[...])
    parts = [p.astype(F32) for p in thirds(columns)]
    lane = iota((ROWS, TILE), 1) % 32
    for j in range(HEADS):
        pair = slice((j // 2) * HEAD_DIM, (j // 2 + 1) * HEAD_DIM)
        own = slice(j * HEAD_DIM, (j + 1) * HEAD_DIM)
        sent_in[j, 0:16, :] = q_ref[:, pair]
        sent_in[j, 16:32, :] = k_ref[:, pair]
        sent_in[j, 32:48, :] = v_ref[:, own]
        sent_in[j, 48:64, :] = g_ref[:, own]
        small = jnp.zeros((ROWS, TILE), F32)
        for n in range(3):
            moved = pltpu.roll(parts[n], (TILE - j + n) % TILE, 1)
            small = jnp.where(lane == n, moved, small)
        sent_in[j, 64:80, :] = small.astype(BF16)
    pl.semaphore_wait(barrier, HEADS - 1 + 2 * len(REACH))
    start_plane(me, device, sent_in, in_ref, plane_send, plane_recv)

    base = lax.div(dp, 4) * SPAN
    lower_ref[...] = (iota((SPAN, SPAN), 0) >= iota((SPAN, SPAN), 1)).astype(F32).astype(BF16)
    upper_ref[...] = (iota((SPAN, SPAN), 0) <= iota((SPAN, SPAN), 1)).astype(F32).astype(BF16)
    start = jnp.full((SPAN, TILE), -base, jnp.int32)
    row = iota((SPAN, TILE), 0)
    bound, last_start = -base, -base
    for n in range(NDOCS - 1):
        bound = bound + lengths_ref[n]
        start = jnp.where(row >= bound, bound, start)
        last_start = jnp.where(bound <= SPAN - 1, bound, last_start)
    start_ref[...] = start
    end_ref[...] = (row >= last_start).astype(F32)
    for size in (TILE, 2 * TILE):
        for n in range(SPAN // (2 * size)):
            top = slice(2 * n * size, (2 * n + 1) * size)
            low = slice((2 * n + 1) * size, (2 * n + 2) * size)
            th_ref[top, low] = jnp.zeros((size, size), BF16)
            tl_ref[top, low] = jnp.zeros((size, size), BF16)
    finish_plane(sent_in, in_ref, plane_send, plane_recv)

    qr, kr, vr, gr, small = raw_parts(in_ref)
    qf, kf = qr.astype(F32), kr.astype(F32)
    pick_row, pick_col = iota((TILE, 3 * TILE), 0), iota((TILE, 3 * TILE), 1)
    pick = (pick_row // 32 == pick_col // TILE) & (pick_row % 32 < 3)
    spread = product(small, pick.astype(F32).astype(BF16))
    beta = jax.nn.sigmoid(spread[:, 0:TILE])
    weight = spread[:, 2 * TILE :]
    sk = lax.rsqrt(jnp.sum(kf * kf, axis=1, keepdims=True) + 1e-06)
    sk = jnp.broadcast_to(sk, (SPAN, TILE))
    csw = lax.rsqrt(jnp.sum(qf * qf, axis=1, keepdims=True) + 1e-06) * SCALE * weight
    running = product(lower_ref[...], small)
    lane = iota((SPAN, TILE), 1)
    running = jnp.where(lane // 32 == 1, running, 0.0)
    cumul = -jnp.broadcast_to(jnp.sum(running, axis=1, keepdims=True), (SPAN, TILE))
    start = start_ref[...]
    gamma = jnp.where(start < 0, jnp.exp(cumul), 0.0)
    last = cumul[SPAN - 1 : SPAN, :]
    end = end_ref[...] * jnp.exp(jnp.minimum(last - cumul, 0.0))
    pack = jnp.where(lane == 0, cumul, jnp.where(lane == 1, sk, 0.0))
    across = jnp.transpose(pack)
    tok, src = iota((TILE, TILE), 0), iota((TILE, TILE), 1)
    for i in range(TILES):
        bi = band(i)
        for j in range(i + 1):
            bj = band(j)
            gap = cumul[bi] - across[0:1, bj]
            seen = src + j * TILE >= start[bi]
            if i == j:
                seen = seen & (tok >= src)
            pair = jnp.where(seen, jnp.exp(jnp.minimum(gap, 0.0)), 0.0) * across[1:2, bj]
            gqk = pair * csw[bi]
            gkk = pair * (beta[bi] * sk[bi])
            if i == j:
                gkk = jnp.where(tok > src, gkk, 0.0)
            gqk_ref[bi, bj] = gqk
            gkk_ref[bi, bj] = gkk
            a_ref[bi, bj] = gkk * product(kr[bi], kr[bj], (1, 1))
            pw_ref[bi, bj] = gqk * product(qr[bi], kr[bj], (1, 1))
    eye = (tok == src).astype(F32)
    inverse = [
        eye - jnp.where(tok // 2 == src // 2, a_ref[band(i), band(i)], 0.0) for i in range(TILES)
    ]
    size = 2
    while size < TILE:
        inside = (tok // (2 * size) == src // (2 * size)) & (tok // size != src // size)
        for i in range(TILES):
            block = halves(jnp.where(inside, a_ref[band(i), band(i)], 0.0))
            parts = halves(inverse[i])
            inverse[i] = inverse[i] - product3(parts, halves(product3(block, parts)))
        size *= 2
    for i in range(TILES):
        th_ref[band(i), band(i)], tl_ref[band(i), band(i)] = halves(inverse[i])
    while size < SPAN:
        for n in range(SPAN // (2 * size)):
            top = slice(2 * n * size, (2 * n + 1) * size)
            low = slice((2 * n + 1) * size, (2 * n + 2) * size)
            right = product3(halves(a_ref[low, top]), (th_ref[top, top], tl_ref[top, top]))
            block = -product3((th_ref[low, low], tl_ref[low, low]), halves(right))
            th_ref[low, top], tl_ref[low, top] = halves(block)
        size *= 2
    keys = sk * kf
    rhs = halves(jnp.concatenate([beta * vr.astype(F32), beta * gamma * keys], axis=1))
    solved = []
    for i in range(TILES):
        bi, upto = band(i), slice(0, (i + 1) * TILE)
        part = product3((th_ref[bi, upto], tl_ref[bi, upto]), (rhs[0][upto], rhs[1][upto]))
        u0_ref[bi] = part[:, :TILE]
        wk_ref[bi] = part[:, TILE:]
        solved.append(part)
    solved = halves(jnp.concatenate(solved, axis=0))
    end_keys = end * keys
    both = product3(solved, halves(end_keys), (0, 0))
    phit = gamma[SPAN - 1 : SPAN, :] * eye - both[TILE:]
    wks = (solved[0][:, TILE:], solved[1][:, TILE:])
    reads = []
    for i in range(TILES):
        bi, upto = band(i), slice(0, (i + 1) * TILE)
        part = product3(halves(pw_ref[bi, upto]), (wks[0][upto], wks[1][upto]))
        reads.append(gamma[bi] * csw[bi] * qf[bi] - part)
    lt = product2r(gr, halves(jnp.concatenate(reads, axis=0)), (0, 0))

    def ship(way, number, source, target, distance):
        copy = pltpu.make_async_remote_copy(
            src_ref=source,
            dst_ref=target,
            send_sem=map_send.at[way, number],
            recv_sem=map_recv.at[way, number],
            device_id=along(distance if way == 0 else -distance),
            device_id_type=MESH,
        )
        copy.start()
        return copy

    copies = []
    maps_out[0, 0, 0:TILE] = phit
    maps_out[0, 0, TILE:] = both[:TILE]
    maps_out[1, 0, 0:TILE] = jnp.transpose(phit)
    maps_out[1, 0, TILE:] = lt
    for way in range(2):
        copies.append(ship(way, 0, maps_out.at[way, 0], maps_in.at[way, 0], 1))
    pulled = []
    for j in range(TILES):
        bj, onward = band(j), slice(j * TILE, SPAN)
        pulled.append(product2l(halves(pw_ref[onward, bj]), gr[onward], (0, 0)))
    pulled = halves(jnp.concatenate([jnp.concatenate(pulled, axis=0), end_keys], axis=1))
    for j in range(TILES):
        bj, onward = band(j), slice(j * TILE, SPAN)
        part = product3(
            (th_ref[onward, bj], tl_ref[onward, bj]), (pulled[0][onward], pulled[1][onward]), (0, 0)
        )
        x0_ref[bj] = part[:, :TILE]
        xk_ref[bj] = part[:, TILE:]
    steps = []
    for way in range(2):
        copies[way].wait_recv()
        own = maps_out[way, 0]
        joined = product3(halves(maps_in[way, 0]), halves(own[:TILE]))
        maps_out[way, 1, 0:TILE] = joined[:TILE]
        maps_out[way, 1, TILE:] = joined[TILE:] + own[TILE:]
        copies.append(ship(way, 1, maps_out.at[way, 1, pl.ds(TILE, TILE)], far_in.at[way, 0], 2))
        steps.append(halves(maps_out[way, 1, 0:TILE]))
    for way in range(2):
        copies.append(ship(way, 4, maps_out.at[way, 1], maps_in.at[way, 1], 1))
    for level in range(2):
        for way in range(2):
            copies[2 + way + 4 * level].wait_recv()
            reached = product3(halves(far_in[way, level]), steps[way])
            far_out[way, level] = reached + maps_out[way, 1, TILE:]
            copies.append(
                ship(way, 2 + level, far_out.at[way, level], far_in.at[way, level + 1], 2 + level)
            )
    ends = []
    for way in range(2):
        copies[4 + way].wait_recv()
        near = maps_in[way, 1]
        step = halves(near[:TILE])
        copies[8 + way].wait_recv()
        ends.append(product3(halves(far_in[way, 2]), step) + near[TILE:])
    state, grad = halves(ends[0]), halves(ends[1])

    u = u0_ref[...] - product3(halves(wk_ref[...]), state, (1, 1))
    x = x0_ref[...] + product3(halves(xk_ref[...]), grad, (1, 1))
    dv = beta * x
    sent_out[:, 16:32, :] = dv.astype(BF16).reshape(HEADS, ROWS, TILE)
    (uh, ul), (xh, xl) = halves(u), halves(x)
    for i in range(TILES):
        bi = band(i)
        for j in range(i + 1):
            bj = band(j)
            read = product2r(gr[bi], (uh[bj], ul[bj]), (1, 1))
            solve = product3((xh[bi], xl[bi]), (uh[bj], ul[bj]), (1, 1))
            fqh_ref[bi, bj], fql_ref[bi, bj] = halves(gqk_ref[bi, bj] * read)
            fkh_ref[bi, bj], fkl_ref[bi, bj] = halves(-gkk_ref[bi, bj] * solve)
    dq = csw * gamma * product2r(gr, state)
    dk = end * sk * product3((uh, ul), grad) - beta * gamma * sk * product3((xh, xl), state)
    for i in range(TILES):
        bi, upto, onward = band(i), slice(0, (i + 1) * TILE), slice(i * TILE, SPAN)
        dirs_ref[0, bi] = dq[bi] + product2l((fqh_ref[bi, upto], fql_ref[bi, upto]), kr[upto])
        part = product2l((fqh_ref[onward, bi], fql_ref[onward, bi]), qr[onward], (0, 0))
        part = part + product2l((fkh_ref[onward, bi], fkl_ref[onward, bi]), kr[onward], (0, 0))
        part = part + product2l((fkh_ref[bi, upto], fkl_ref[bi, upto]), kr[upto])
        dirs_ref[1, bi] = dk[bi] + part
    pair = pltpu.make_async_remote_copy(
        src_ref=dirs_ref.at[1 - core],
        dst_ref=partner_in,
        send_sem=pair_send,
        recv_sem=pair_recv,
        device_id=(dp, head + 1 - 2 * core),
        device_id_type=MESH,
    )
    pair.start()
    after = product3(state, halves(phit)) + both[:TILE]
    total = jnp.sum(jnp.sum(ends[1] * after, axis=1, keepdims=True), axis=0, keepdims=True)
    xu = jnp.sum(x * u, axis=1, keepdims=True)
    change = jnp.sum(
        qf * dirs_ref[0] - kf * dirs_ref[1] - 2.0 * (vr.astype(F32) * dv), axis=1, keepdims=True
    )
    change = change + 2.0 * xu
    change = jnp.where(iota((SPAN, 1), 0) == SPAN - 1, change + total, change)
    pieces = [p.astype(F32) for p in thirds(jnp.broadcast_to(change, (SPAN, TILE)))]
    packed = jnp.zeros((SPAN, TILE), F32)
    for n in range(3):
        packed = jnp.where(lane == n, pieces[n], packed)
    ddecay = -jnp.sum(product(upper_ref[...], packed.astype(BF16)), axis=1, keepdims=True)
    ddecay = jnp.broadcast_to(ddecay, (SPAN, TILE))
    out = jnp.zeros((SPAN, TILE), F32)
    for n, values in enumerate((xu * (1.0 - beta), ddecay)):
        high, low = halves(values)
        out = jnp.where(lane == me + 32 * n, high.astype(F32), out)
        out = jnp.where(lane == me + 32 * n + 64, low.astype(F32), out)
    sent_out[:, 32:48, :] = out.astype(BF16).reshape(HEADS, ROWS, TILE)
    own = jnp.where(core == 0, qf, kf)
    inverse = 1.0 / (jnp.sum(own * own, axis=1, keepdims=True) + 1e-06)
    pair.wait_recv()
    part = dirs_ref[core] + partner_in[...]
    part = part - own * (jnp.sum(own * part, axis=1, keepdims=True) * inverse)
    sent_out[:, 0:16, :] = part.astype(BF16).reshape(HEADS, ROWS, TILE)
    start_plane(me, device, sent_out, landed, out_send, out_recv)
    for one in copies:
        one.wait_send()
    pair.wait_send()
    finish_plane(sent_out, landed, out_send, out_recv)
    out_ref[...] = landed[...]


def unpack(in_ref, dq_ref, dk_ref, dv_ref, db_ref, dd_ref):
    total = jnp.zeros((ROWS, TILE), F32)
    for j in range(HEADS):
        to_ref = (dq_ref, dk_ref)[j % 2]
        to_ref[:, (j // 2) * HEAD_DIM : (j // 2 + 1) * HEAD_DIM] = in_ref[j, 0:16, :]
        dv_ref[:, j * HEAD_DIM : (j + 1) * HEAD_DIM] = in_ref[j, 16:32, :]
        total = total + in_ref[j, 32:48, :].astype(F32)
    total = total + pltpu.roll(total, 64, 1)
    db_ref[...] = total[:, 0:32]
    dd_ref[...] = total[:, 32:64]


def shards(query, key, value, beta_logit, decay, out_grad, ratio, clip_mask, lengths):
    dma = pltpu.SemaphoreType.DMA
    vmem, smem = [pl.BlockSpec(memory_space=m) for m in (pltpu.VMEM, pltpu.SMEM)]
    square, tall, big = (TILE, TILE), (SPAN, TILE), (SPAN, SPAN)
    block_in, block_out, double = (HEADS, 80, TILE), (HEADS, 48, TILE), (2 * TILE, TILE)
    blocks = pl.pallas_call(
        whole,
        out_shape=jax.ShapeDtypeStruct(block_out, BF16),
        in_specs=[vmem] * 8 + [smem],
        out_specs=vmem,
        scratch_shapes=[
            pltpu.VMEM(block_in, BF16),
            pltpu.VMEM(block_in, BF16),
            pltpu.VMEM((ROWS, TILE), F32),
            pltpu.VMEM(big, BF16),
            pltpu.VMEM(big, BF16),
            pltpu.VMEM(tall, jnp.int32),
            pltpu.VMEM(tall, F32),
        ]
        + [pltpu.VMEM(tall, F32)] * 4
        + [pltpu.VMEM(big, F32)] * 4
        + [pltpu.VMEM(big, BF16)] * 6
        + [
            pltpu.VMEM((2,) + tall, F32),
            pltpu.VMEM(tall, F32),
            pltpu.VMEM(block_out, BF16),
            pltpu.VMEM(block_out, BF16),
            pltpu.VMEM((2, 2) + double, F32),
            pltpu.VMEM((2, 2) + double, F32),
            pltpu.VMEM((2, 2) + square, F32),
            pltpu.VMEM((2, 3) + square, F32),
        ]
        + [dma] * 6
        + [dma((2, 5)), dma((2, 5))],
        compiler_params=pltpu.CompilerParams(
            vmem_limit_bytes=LIMIT, collective_id=0, has_side_effects=True
        ),
        cost_estimate=pl.CostEstimate(flops=1 << 30, bytes_accessed=1 << 20, transcendentals=0),
        name="whole",
    )(
        query, key, value, out_grad, beta_logit, decay,
        ratio.reshape(1, ROWS), clip_mask.reshape(1, ROWS), lengths,
    )
    wide = HEADS * HEAD_DIM
    shapes = [((ROWS, wide // 2), BF16)] * 2 + [((ROWS, wide), BF16)] + [((ROWS, HEADS), F32)] * 2
    return tuple(
        pl.pallas_call(
            unpack,
            out_shape=[jax.ShapeDtypeStruct(s, d) for s, d in shapes],
            in_specs=[vmem],
            out_specs=[vmem] * 5,
            compiler_params=pltpu.CompilerParams(vmem_limit_bytes=LIMIT),
            cost_estimate=pl.CostEstimate(flops=0, bytes_accessed=1 << 20, transcendentals=0),
            name="unpack",
        )(blocks)
    )


def solution(mesh):
    split = P(("dp", "head"), None)
    line = P(("dp", "head"))
    return jax.shard_map(
        shards,
        mesh=mesh,
        in_specs=(split,) * 6 + (line, line, P()),
        out_specs=(split,) * 5,
        check_vma=False,
    )
```

```python
import jax
import jax.numpy as jnp
from jax import lax
from jax.experimental import pallas as pl
from jax.experimental.pallas import tpu as pltpu
from jax.sharding import PartitionSpec as P

HEAD_DIM = 128
TILE = 128
HEADS = 32
ROWS = 16
SPAN = HEADS * ROWS
TILES = SPAN // TILE
HALF = SPAN // 2
CHUNKS = 4
REACH = (1, 2)
NDOCS = 16
SCALE = HEAD_DIM ** (-0.5)
MESH = pl.DeviceIdType.MESH
F32 = jnp.float32
BF16 = jnp.bfloat16
LIMIT = 56 * 1024 * 1024


def product(left, right, over=(1, 0)):
    return lax.dot_general(
        left, right, (((over[0],), (over[1],)), ((), ())), preferred_element_type=F32
    )


def halves(values):
    high = values.astype(BF16)
    return high, (values - high.astype(F32)).astype(BF16)


def thirds(values):
    high = values.astype(BF16)
    rest = values - high.astype(F32)
    middle = rest.astype(BF16)
    return high, middle, (rest - middle.astype(F32)).astype(BF16)


def joined(parts, axis):
    return jnp.concatenate(parts, axis=axis)


def product3(left, right, over=(1, 0)):
    (lh, ll), (rh, rl) = left, right
    return product(joined([lh, ll, lh], over[0]), joined([rh, rh, rl], over[1]), over)


def product2l(left, right, over=(1, 0)):
    return product(joined(left, over[0]), joined([right, right], over[1]), over)


def product2r(left, right, over=(1, 0)):
    return product(joined([left, left], over[0]), joined(right, over[1]), over)


def iota(shape, axis):
    return lax.broadcasted_iota(jnp.int32, shape, axis)


def band(index, size=TILE):
    return slice(index * size, (index + 1) * size)


def place():
    dp, head = lax.axis_index("dp"), lax.axis_index("head")
    base = lax.div(dp, 4) * 4
    me = lax.rem(dp, 4) * 8 + head

    def device(index):
        return (base + lax.div(index, 8), lax.rem(index, 8))

    return dp, head, me, device


def greet_plane(me, device):
    barrier = pltpu.get_barrier_semaphore()

    def greet(offset, carry):
        target = lax.rem(me + offset, HEADS)
        pl.semaphore_signal(barrier, inc=1, device_id=device(target), device_id_type=MESH)
        return carry

    lax.fori_loop(1, HEADS, greet, 0)
    return barrier


def start_plane(me, device, kinds):
    def send(offset, carry):
        target = lax.rem(me + 7 * offset, HEADS)
        for sent, landed, send_sem, recv_sem in kinds:
            pltpu.make_async_remote_copy(
                src_ref=sent.at[target],
                dst_ref=landed.at[me],
                send_sem=send_sem,
                recv_sem=recv_sem,
                device_id=device(target),
                device_id_type=MESH,
            ).start()
        return carry

    lax.fori_loop(1, HEADS, send, 0)
    for sent, landed, _, _ in kinds:
        landed[me] = sent[me]


def await_sent(kinds):
    others = pl.ds(0, HEADS - 1)
    for sent, landed, send_sem, _ in kinds:
        pltpu.make_async_copy(sent.at[others], landed.at[others], send_sem).wait()


def await_landed(kinds):
    others = pl.ds(0, HEADS - 1)
    for sent, landed, _, recv_sem in kinds:
        pltpu.make_async_copy(sent.at[others], landed.at[others], recv_sem).wait()


def rows_of(landed):
    return landed.reshape(SPAN, TILE)


def prepare(base, lengths_ref, m):
    down, along = iota((SPAN, SPAN), 0), iota((SPAN, SPAN), 1)
    m.lower[...] = (down >= along).astype(F32).astype(BF16)
    m.upper[...] = (down <= along).astype(F32).astype(BF16)
    down, along = iota((HEADS, SPAN), 0), iota((HEADS, SPAN), 1)
    m.fold[...] = (down == along // ROWS).astype(F32).astype(BF16)
    down, along = iota((SPAN, HEADS), 0), iota((SPAN, HEADS), 1)
    m.unfold[...] = (down // ROWS == along).astype(F32).astype(BF16)
    start = jnp.full((SPAN, TILE), -base, jnp.int32)
    row = iota((SPAN, TILE), 0)
    bound, last_start = -base, -base
    for n in range(NDOCS - 1):
        bound = bound + lengths_ref[n]
        start = jnp.where(row >= bound, bound, start)
        last_start = jnp.where(bound <= SPAN - 1, bound, last_start)
    m.start[...] = start
    m.end[...] = (row >= last_start).astype(F32)
    for size in (TILE, HALF):
        for n in range(SPAN // (2 * size)):
            top, low = band(2 * n, size), band(2 * n + 1, size)
            m.th[top, low] = jnp.zeros((size, size), BF16)
            m.tl[top, low] = jnp.zeros((size, size), BF16)


def first_keys(m):
    kr = rows_of(m.k_in[...])
    kf = kr.astype(F32)
    lane, row = iota((SPAN, TILE), 1), iota((SPAN, TILE), 0)
    high, low = halves(m.rows_in[:, 0, :])
    packed = (high.astype(F32) + pltpu.roll(low.astype(F32), 64, 1)).astype(BF16)
    small = product(m.unfold[...], packed)
    small = jnp.where(lane % ROWS == row % ROWS, small, 0.0).astype(BF16)
    pick_row, pick_col = iota((TILE, 3 * TILE), 0), iota((TILE, 3 * TILE), 1)
    pick = ((pick_row // ROWS) % 4 == pick_col // TILE).astype(F32).astype(BF16)
    spread = product(small, pick)
    beta = jax.nn.sigmoid(spread[:, 0:TILE])
    m.weight[...] = spread[:, 2 * TILE :]
    sk = lax.rsqrt(jnp.sum(kf * kf, axis=1, keepdims=True) + 1e-06)
    sk = jnp.broadcast_to(sk, (SPAN, TILE))
    running = product(m.lower[...], small)
    running = jnp.where((lane // ROWS) % 4 == 1, running, 0.0)
    cumul = -jnp.broadcast_to(jnp.sum(running, axis=1, keepdims=True), (SPAN, TILE))
    start = m.start[...]
    gamma = jnp.where(start < 0, jnp.exp(cumul), 0.0)
    last = cumul[SPAN - 1 : SPAN, :]
    m.end[...] = m.end[...] * jnp.exp(jnp.minimum(last - cumul, 0.0))
    m.beta[...] = beta
    m.gamma[...] = gamma
    m.sk[...] = sk
    pack = jnp.where(lane == 0, cumul, jnp.where(lane == 1, sk, 0.0))
    across = jnp.transpose(pack)
    tok, src = iota((TILE, TILE), 0), iota((TILE, TILE), 1)
    for i in range(TILES):
        bi = band(i)
        for j in range(i + 1):
            bj = band(j)
            gap = cumul[bi] - across[0:1, bj]
            seen = src + j * TILE >= start[bi]
            if i == j:
                seen = seen & (tok >= src)
            pair = jnp.where(seen, jnp.exp(jnp.minimum(gap, 0.0)), 0.0) * across[1:2, bj]
            gkk = pair * (beta[bi] * sk[bi])
            if i == j:
                gkk = jnp.where(tok > src, gkk, 0.0)
            m.gqk[bi, bj] = pair
            m.gkk[bi, bj] = gkk
            m.a[bi, bj] = gkk * product(kr[bi], kr[bj], (1, 1))
    eye = (tok == src).astype(F32)
    inverse = [
        eye - jnp.where(tok // 2 == src // 2, m.a[band(i), band(i)], 0.0) for i in range(TILES)
    ]
    size = 2
    while size < TILE:
        inside = (tok // (2 * size) == src // (2 * size)) & (tok // size != src // size)
        for i in range(TILES):
            block = halves(jnp.where(inside, m.a[band(i), band(i)], 0.0))
            parts = halves(inverse[i])
            inverse[i] = inverse[i] - product3(parts, halves(product3(block, parts)))
        size *= 2
    for i in range(TILES):
        m.th[band(i), band(i)], m.tl[band(i), band(i)] = halves(inverse[i])


def first_state(m):
    kr, vr = rows_of(m.k_in[...]), rows_of(m.v_in[...])
    beta, gamma = m.beta[...], m.gamma[...]
    size = TILE
    while size < SPAN:
        for n in range(SPAN // (2 * size)):
            top, low = band(2 * n, size), band(2 * n + 1, size)
            right = product3(halves(m.a[low, top]), (m.th[top, top], m.tl[top, top]))
            block = -product3((m.th[low, low], m.tl[low, low]), halves(right))
            m.th[low, top], m.tl[low, top] = halves(block)
        size *= 2
    keys = m.sk[...] * kr.astype(F32)
    rhs = halves(joined([beta * vr.astype(F32), beta * gamma * keys], 1))
    solved = []
    for i in range(2):
        bi, upto = band(i, HALF), slice(0, (i + 1) * HALF)
        part = product3((m.th[bi, upto], m.tl[bi, upto]), (rhs[0][upto], rhs[1][upto]))
        m.u0[bi] = part[:, :TILE]
        m.wk[bi] = part[:, TILE:]
        solved.append(part)
    ends = halves(m.end[...] * keys)
    m.zh[:, TILE:], m.zl[:, TILE:] = ends
    both = product3(halves(joined(solved, 0)), ends, (0, 0))
    eye = (iota((TILE, TILE), 0) == iota((TILE, TILE), 1)).astype(F32)
    return gamma[SPAN - 1 : SPAN, :] * eye - both[TILE:], both[:TILE]


def first_grad(m):
    kr, qr, gr = [rows_of(r[...]) for r in (m.k_in, m.q_in, m.g_in)]
    qf = qr.astype(F32)
    csw = lax.rsqrt(jnp.sum(qf * qf, axis=1, keepdims=True) + 1e-06) * SCALE * m.weight[...]
    m.csw[...] = csw
    for i in range(TILES):
        bi = band(i)
        for j in range(i + 1):
            bj = band(j)
            gqk = m.gqk[bi, bj] * csw[bi]
            m.gqk[bi, bj] = gqk
            m.ph[bi, bj], m.pl[bi, bj] = halves(gqk * product(qr[bi], kr[bj], (1, 1)))
    for j in range(TILES):
        bj, onward = band(j), slice(j * TILE, SPAN)
        pulled = product2l((m.ph[onward, bj], m.pl[onward, bj]), gr[onward], (0, 0))
        m.zh[bj, :TILE], m.zl[bj, :TILE] = halves(pulled)
    reads = product2r(gr, halves(m.gamma[...] * csw * qf), (0, 0))
    return reads - product3((m.zh[:, :TILE], m.zl[:, :TILE]), halves(m.wk[...]), (0, 0))


def first_beside(m):
    for j in range(2):
        bj, onward = band(j, HALF), slice(j * HALF, SPAN)
        part = product3((m.th[onward, bj], m.tl[onward, bj]), (m.zh[onward], m.zl[onward]), (0, 0))
        m.x0[bj] = part[:, :TILE]
        m.xk[bj] = part[:, TILE:]


def second(m, state_t, grad_t, phit, bt, send_values, send_directions, finish_directions, send_rows):
    kr, qr, vr, gr = [rows_of(r[...]) for r in (m.k_in, m.q_in, m.v_in, m.g_in)]
    beta, gamma, sk, csw, end = m.beta[...], m.gamma[...], m.sk[...], m.csw[...], m.end[...]
    state, grad = halves(state_t), halves(grad_t)
    x = m.x0[...] + product3(halves(m.xk[...]), grad, (1, 1))
    dv = beta * x
    send_values(dv)
    u = m.u0[...] - product3(halves(m.wk[...]), state, (1, 1))
    (uh, ul), (xh, xl) = halves(u), halves(x)
    for i in range(TILES):
        bi = band(i)
        for j in range(i + 1):
            bj = band(j)
            read = product2r(gr[bi], (uh[bj], ul[bj]), (1, 1))
            solve = product3((xh[bi], xl[bi]), (uh[bj], ul[bj]), (1, 1))
            m.fqh[bi, bj], m.fql[bi, bj] = halves(m.gqk[bi, bj] * read)
            m.fkh[bi, bj], m.fkl[bi, bj] = halves(-m.gkk[bi, bj] * solve)
    dq = csw * gamma * product2r(gr, state)
    dk = end * sk * product3((uh, ul), grad) - beta * gamma * sk * product3((xh, xl), state)
    for i in range(TILES):
        bi, upto, onward = band(i), slice(0, (i + 1) * TILE), slice(i * TILE, SPAN)
        m.dirs[0, bi] = dq[bi] + product2l((m.fqh[bi, upto], m.fql[bi, upto]), kr[upto])
        part = product2l((m.fqh[onward, bi], m.fql[onward, bi]), qr[onward], (0, 0))
        part = part + product2l((m.fkh[onward, bi], m.fkl[onward, bi]), kr[onward], (0, 0))
        part = part + product2l((m.fkh[bi, upto], m.fkl[bi, upto]), kr[upto])
        m.dirs[1, bi] = dk[bi] + part
    send_directions()
    qf, kf = qr.astype(F32), kr.astype(F32)
    after = product3(state, halves(phit)) + bt
    total = jnp.sum(jnp.sum(grad_t * after, axis=1, keepdims=True), axis=0, keepdims=True)
    xu = jnp.sum(x * u, axis=1, keepdims=True)
    change = jnp.sum(
        qf * m.dirs[0] - kf * m.dirs[1] - 2.0 * (vr.astype(F32) * dv), axis=1, keepdims=True
    )
    change = change + 2.0 * xu
    change = jnp.where(iota((SPAN, 1), 0) == SPAN - 1, change + total, change)
    lane, row = iota((SPAN, TILE), 1), iota((SPAN, TILE), 0)
    pieces = [p.astype(F32) for p in thirds(jnp.broadcast_to(change, (SPAN, TILE)))]
    packed = jnp.zeros((SPAN, TILE), F32)
    for n in range(3):
        packed = jnp.where(lane == n, pieces[n], packed)
    ddecay = -jnp.sum(product(m.upper[...], packed.astype(BF16)), axis=1, keepdims=True)
    ddecay = jnp.broadcast_to(ddecay, (SPAN, TILE))
    out = jnp.where(lane == row % ROWS, xu * (1.0 - beta), 0.0)
    out = jnp.where(lane == row % ROWS + ROWS, ddecay, out)
    high, middle, low = thirds(out)
    fold = m.fold[...]
    lines = product(fold, high) + product(fold, middle) + product(fold, low)
    send_rows(lines)
    finish_directions(qf, kf)


class Memory:
    def __init__(self, **refs):
        self.__dict__.update(refs)


def scratch():
    dma = pltpu.SemaphoreType.DMA
    square, tall, big = (TILE, TILE), (SPAN, TILE), (SPAN, SPAN)
    part, lines, double = (HEADS, ROWS, TILE), (HEADS, 1, TILE), (2 * TILE, TILE)
    shapes = dict(
        columns=((TILE, TILE), F32),
        lower=(big, BF16), upper=(big, BF16), fold=((HEADS, SPAN), BF16), unfold=((SPAN, HEADS), BF16),
        start=(tall, jnp.int32), end=(tall, F32), weight=(tall, F32),
        beta=(tall, F32), gamma=(tall, F32), sk=(tall, F32), csw=(tall, F32),
        u0=(tall, F32), wk=(tall, F32), x0=(tall, F32), xk=(tall, F32),
        gqk=(big, F32), gkk=(big, F32), a=(big, F32),
        th=(big, BF16), tl=(big, BF16), ph=(big, BF16), pl=(big, BF16),
        fqh=(big, BF16), fql=(big, BF16), fkh=(big, BF16), fkl=(big, BF16),
        zh=((SPAN, 2 * TILE), BF16), zl=((SPAN, 2 * TILE), BF16),
        dirs=((2,) + tall, F32), partner=(tall, F32),
        maps_out=((2,) + double, F32), maps_in=((2,) + double, F32),
        far_out=((2, 3) + square, F32), far_in=((2, 4) + square, F32),
        q_here=((ROWS, HEADS * TILE // 2), BF16), k_here=((ROWS, HEADS * TILE // 2), BF16),
        v_here=((ROWS, HEADS * TILE), BF16), g_here=((ROWS, HEADS * TILE), BF16),
        beta_here=((ROWS, HEADS), F32), decay_here=((ROWS, HEADS), F32),
        ratio_here=((1, ROWS), F32), clip_here=((1, ROWS), jnp.int32),
    )
    for name in "kqvgdp":
        shapes[name + "_out"] = (part, BF16)
        shapes[name + "_in"] = (part, BF16)
    for name in ("rows", "back"):
        shapes[name + "_out"] = (lines, F32)
        shapes[name + "_in"] = (lines, F32)
    memory = {name: pltpu.VMEM(*shape) for name, shape in shapes.items()}
    memory.update(
        plane_send=dma((8,)), plane_recv=dma((8,)), map_send=dma((2, 2 + 4 * CHUNKS)), map_recv=dma((2, 2 + 4 * CHUNKS)),
        pair_send=dma((TILES,)), pair_recv=dma((TILES,)), here=dma((8,)),
    )
    return memory


def whole(
    q_ref, k_ref, v_ref, g_ref, beta_ref, decay_ref, ratio_ref, clip_ref, lengths_ref,
    dirs_ref, values_ref, lines_ref, *refs,
):
    m = Memory(**dict(zip(scratch(), refs)))
    dp, head, me, device = place()
    count, core = lax.axis_size("dp"), lax.rem(head, 2)

    def along(distance):
        return (lax.rem(dp + (count + 4 * distance), count), head)

    barrier = greet_plane(me, device)
    for distance in REACH:
        for sign in (1, -1):
            pl.semaphore_signal(
                barrier, inc=1, device_id=along(sign * distance), device_id_type=MESH
            )

    names = ("k", "beta", "decay", "ratio", "clip", "v", "q", "g")
    sources = (k_ref, beta_ref, decay_ref, ratio_ref, clip_ref, v_ref, q_ref, g_ref)
    local = {}
    for n, (name, source) in enumerate(zip(names, sources)):
        local[name] = pltpu.make_async_copy(source, getattr(m, name + "_here"), m.here.at[n])
        local[name].start()

    kinds = (("k", "rows"), ("v",), ("q", "g"), ("d",), ("back",), ("p",))
    number = {name: n for n, name in enumerate(n for kind in kinds for n in kind)}

    def kind_of(index):
        return [
            (getattr(m, n + "_out"), getattr(m, n + "_in"), m.plane_send.at[number[n]], m.plane_recv.at[number[n]])
            for n in kinds[index]
        ]

    m.columns[...] = jnp.zeros((TILE, TILE), F32)
    for name in names[:5]:
        local[name].wait()
    m.columns[0:ROWS, 0:HEADS] = m.beta_here[...]
    m.columns[ROWS : 2 * ROWS, 0:HEADS] = m.decay_here[...]
    weight = m.ratio_here[...] * m.clip_here[...].astype(F32)
    turned = jnp.transpose(m.columns[...])[0:HEADS]
    m.columns[0:HEADS, :] = turned
    m.columns[0:HEADS, 2 * ROWS : 3 * ROWS] = jnp.broadcast_to(weight, (HEADS, ROWS))
    for j in range(HEADS):
        m.k_out[j] = m.k_here[:, band(j // 2)]
        m.rows_out[j] = m.columns[j : j + 1, :]
    pl.semaphore_wait(barrier, HEADS - 1 + 2 * len(REACH))
    start_plane(me, device, kind_of(0))
    local["v"].wait()
    for j in range(HEADS):
        m.v_out[j] = m.v_here[:, band(j)]
    await_sent(kind_of(0))
    start_plane(me, device, kind_of(1))
    prepare(lax.div(dp, 4) * SPAN, lengths_ref, m)
    local["q"].wait()
    local["g"].wait()
    for j in range(HEADS):
        m.q_out[j] = m.q_here[:, band(j // 2)]
        m.g_out[j] = m.g_here[:, band(j)]
    await_sent(kind_of(1))
    start_plane(me, device, kind_of(2))
    await_landed(kind_of(0))
    first_keys(m)
    await_landed(kind_of(1))

    copies = {}

    def ship(way, slot, source, target, distance):
        copies[way, slot] = pltpu.make_async_remote_copy(
            src_ref=source,
            dst_ref=target,
            send_sem=m.map_send.at[way, slot],
            recv_sem=m.map_recv.at[way, slot],
            device_id=along(distance if way == 0 else -distance),
            device_id_type=MESH,
        )
        copies[way, slot].start()

    def ship_half(way, half, value):
        rows = pl.ds(half * TILE, TILE)
        m.maps_out[way, rows] = value
        ship(way, half, m.maps_out.at[way, rows], m.maps_in.at[way, rows], 1)

    def ship_chunk(way, level, chunk, source):
        rows = pl.ds(chunk * (TILE // CHUNKS), TILE // CHUNKS)
        ship(way, 2 + level * CHUNKS + chunk, source.at[rows], m.far_in.at[way, level, rows], 2)

    def ship_bias(way, value):
        ship_half(way, 1, value)
        for chunk in range(CHUNKS):
            ship_chunk(way, 0, chunk, m.maps_out.at[way, pl.ds(TILE, TILE)])

    phit, bt = first_state(m)
    ship_half(0, 0, phit)
    ship_half(1, 0, jnp.transpose(phit))
    ship_bias(0, bt)
    await_landed(kind_of(2))
    lt = first_grad(m)
    ship_bias(1, lt)
    first_beside(m)
    near, steps, biases = [], [], []
    for way in range(2):
        copies[way, 0].wait_recv()
        near.append(halves(m.maps_in[way, 0:TILE]))
        own = halves(m.maps_out[way, 0:TILE])
        steps.append(halves(product3(near[way], own)))
    for way in range(2):
        copies[way, 1].wait_recv()
        own = halves(m.maps_out[way, 0:TILE])
        biases.append(product3(halves(m.maps_in[way, TILE:]), own) + m.maps_out[way, TILE:])
    ends = [[], []]
    for level in range(4):
        for chunk in range(CHUNKS):
            rows = band(chunk, TILE // CHUNKS)
            for way in range(2):
                copies[way, 2 + level * CHUNKS + chunk].wait_recv()
                arrived = halves(m.far_in[way, level, rows])
                if level < 3:
                    m.far_out[way, level, rows] = product3(arrived, steps[way]) + biases[way][rows]
                    ship_chunk(way, level + 1, chunk, m.far_out.at[way, level])
                else:
                    bias = m.maps_in[way, TILE + chunk * (TILE // CHUNKS) :][: TILE // CHUNKS]
                    ends[way].append(product3(arrived, near[way]) + bias)
    ends = [joined(pieces, 0) for pieces in ends]

    def send_values(dv):
        m.d_out[...] = dv.astype(BF16).reshape(HEADS, ROWS, TILE)
        start_plane(me, device, kind_of(3))

    pairs = []

    def send_directions():
        pairs.append(
            pltpu.make_async_remote_copy(
                src_ref=m.dirs.at[1 - core],
                dst_ref=m.partner,
                send_sem=m.pair_send.at[0],
                recv_sem=m.pair_recv.at[0],
                device_id=(dp, head + 1 - 2 * core),
                device_id_type=MESH,
            )
        )
        pairs[-1].start()

    def finish_directions(qf, kf):
        own = jnp.where(core == 0, qf, kf)
        inverse = 1.0 / (jnp.sum(own * own, axis=1, keepdims=True) + 1e-06)
        for pair in pairs:
            pair.wait_recv()
        part = m.dirs[core] + m.partner[...]
        part = part - own * (jnp.sum(own * part, axis=1, keepdims=True) * inverse)
        m.p_out[...] = part.astype(BF16).reshape(HEADS, ROWS, TILE)
        start_plane(me, device, kind_of(5))

    def send_rows(lines):
        for j in range(HEADS):
            m.back_out[j] = lines[j : j + 1, :]
        start_plane(me, device, kind_of(4))

    second(
        m, ends[0], ends[1], phit, bt, send_values, send_directions, finish_directions, send_rows
    )
    for one in list(copies.values()) + pairs:
        one.wait_send()
    for index in (2, 3, 4, 5):
        await_sent(kind_of(index))
    await_landed(kind_of(3))
    values_ref[...] = m.d_in[...]
    await_landed(kind_of(5))
    dirs_ref[...] = m.p_in[...]
    await_landed(kind_of(4))
    lines_ref[...] = m.back_in[...]


def unpack(dirs_ref, values_ref, lines_ref, dq_ref, dk_ref, dv_ref, db_ref, dd_ref):
    for j in range(HEADS):
        to_ref = (dq_ref, dk_ref)[j % 2]
        to_ref[:, band(j // 2)] = dirs_ref[j]
        dv_ref[:, band(j)] = values_ref[j]
    lines = joined([lines_ref[:, 0, :], jnp.zeros((TILE - HEADS, TILE), F32)], 0)
    turned = jnp.transpose(lines)
    db_ref[...] = turned[0:ROWS, 0:HEADS]
    dd_ref[...] = turned[ROWS : 2 * ROWS, 0:HEADS]


def shards(query, key, value, beta_logit, decay, out_grad, ratio, clip_mask, lengths):
    vmem, smem = [pl.BlockSpec(memory_space=m) for m in (pltpu.VMEM, pltpu.SMEM)]
    part, lines = (HEADS, ROWS, TILE), (HEADS, 1, TILE)
    blocks = pl.pallas_call(
        whole,
        out_shape=[jax.ShapeDtypeStruct(s, d) for s, d in ((part, BF16), (part, BF16), (lines, F32))],
        in_specs=[pl.BlockSpec(memory_space=pl.ANY)] * 8 + [smem],
        out_specs=[vmem] * 3,
        scratch_shapes=list(scratch().values()),
        compiler_params=pltpu.CompilerParams(
            vmem_limit_bytes=LIMIT, collective_id=0, has_side_effects=True
        ),
        cost_estimate=pl.CostEstimate(flops=1 << 30, bytes_accessed=1 << 20, transcendentals=0),
        name="whole",
    )(
        query, key, value, out_grad, beta_logit, decay,
        ratio.reshape(1, ROWS), clip_mask.reshape(1, ROWS), lengths,
    )
    wide = HEADS * HEAD_DIM
    shapes = [((ROWS, wide // 2), BF16)] * 2 + [((ROWS, wide), BF16)] + [((ROWS, HEADS), F32)] * 2
    return tuple(
        pl.pallas_call(
            unpack,
            out_shape=[jax.ShapeDtypeStruct(s, d) for s, d in shapes],
            in_specs=[vmem] * 3,
            out_specs=[vmem] * 5,
            compiler_params=pltpu.CompilerParams(vmem_limit_bytes=LIMIT),
            cost_estimate=pl.CostEstimate(flops=0, bytes_accessed=1 << 20, transcendentals=0),
            name="unpack",
        )(*blocks)
    )


def solution(mesh):
    split = P(("dp", "head"), None)
    line = P(("dp", "head"))
    return jax.shard_map(
        shards,
        mesh=mesh,
        in_specs=(split,) * 6 + (line, line, P()),
        out_specs=(split,) * 5,
        check_vma=False,
    )
```
